32 devices in a mesh: row: 8 (over y, x, core), orb: 4 (over z).
Axes of the slice: x: 2, y: 2, z: 4, core: 2. Of those that a mesh axis runs over, the one named last changes fastest.
Arguments:
- chol_vectors: bfloat16 [4, 8192, 8192], P(None, 'row', 'orb'), may hold values from -6 to 6
- orbitals: bfloat16 [8192, 1024], P('orb'), may hold values from -0.0078125 to 0.0078125
Outputs:
- exchange: float32 [8192, 8192], P(('row', 'orb'))
The draws below stay inside these ranges and needn't reach their ends.
All inputs are finite; a program needn't handle non-finite values.
Results may differ from the reference program's by a relative error of at most 0.0032.
Values may be sent and summed in bfloat16 or wider, within the bound.
A program may use at most 128 MiB of HBM per device.

```python
import jax
import jax.numpy as jnp
from jax import lax

NB = 8192
NO = 1024
NCHOL = 4


def shard_levels(key, dims, pieces, least, top_value):
    def one(axis_at, parts):
        heights = jax.random.uniform(jax.random.fold_in(jax.random.fold_in(key, 6), axis_at), (parts,), jnp.float32, least / len(pieces), top_value / len(pieces))
        return jnp.repeat(jnp.exp(heights), dims[axis_at] // parts).reshape((-1,) + (1,) * (len(dims) - axis_at - 1))

    gain = one(*pieces[0])
    for cut in pieces[1:]:
        gain = gain * one(*cut)
    return gain


def gaussian(own_key, extent, width, limit, shards=(), kind=jnp.bfloat16):
    loudness = shard_levels(own_key, extent, shards, -0.22, 0.18) if shards else 1.0
    drawn = jax.random.normal(own_key, extent, jnp.float32) * width * loudness
    return jnp.minimum(jnp.maximum(drawn, -limit), limit).astype(kind)


def setup_inputs(seed: int = 0) -> dict:
    key_list = jax.random.split(jax.random.key(seed), 3)
    return {
        "chol_vectors": gaussian(key_list[0], (NCHOL, NB, NB), 1.0, 6.0, ((1, 8), (2, 4))),
        "orbitals": gaussian(key_list[1], (NB, NO), (NB * 64) ** -0.5, 0.0078125, ((0, 4),)),
    }


def reference(chol_vectors, orbitals):
    coeffs = orbitals.astype(jnp.float32)
    exchange = jnp.zeros((NB, NB), jnp.float32)
    for vector in range(NCHOL):
        half_vec = jnp.dot(chol_vectors[vector].astype(jnp.float32), coeffs, precision=lax.Precision.HIGHEST)
        half_vec = half_vec.astype(jnp.bfloat16).astype(jnp.float32)
        exchange = exchange + jnp.dot(half_vec, half_vec.T, precision=lax.Precision.HIGHEST)
    return exchange
```

```python
import functools

import jax
import jax.numpy as jnp
from jax import lax
from jax.experimental import pallas as pl
from jax.experimental.pallas import tpu as pltpu
from jax.sharding import PartitionSpec as P

MESH = pl.DeviceIdType.MESH
CORES = 2
SPLIT = 2


def snake(place, count):
    half = count // 2
    return place + (place // half) * (half + count - 1 - 2 * place)


def gather_kernel(
    sizes, terms, own, out, stage, landed,
    sum_s, sum_r, up_s, down_s, line_r, ring_s, ring_r, pair_s, pair_r, local_s,
):
    row_n, orb_n, split = sizes
    chips = row_n // CORES
    vectors, block, count = own.shape
    width = count // split
    chunks = vectors * split
    row, z = lax.axis_index("row"), lax.axis_index("orb")
    core = row % CORES
    place = snake(row // CORES, chips)

    def at(step):
        return snake((place + step + chips) % chips, chips) * CORES + core

    onward, back = at(1), at(-1)
    other = row + 1 - 2 * core

    barrier = pltpu.get_barrier_semaphore()
    peers = [(row, (z + d) % orb_n) for d in range(1, orb_n)]
    peers += [(onward, z), (back, z), (other, z)]
    for peer in peers:
        pl.semaphore_signal(barrier, inc=1, device_id=peer, device_id_type=MESH)
    pl.semaphore_wait(barrier, len(peers))

    def columns(k):
        return pl.ds(pl.multiple_of(k * width, width), width)

    def part(k, r, q):
        return out.at[pl.ds(pl.multiple_of((r * orb_n + q) * block, block), block), columns(k)]

    def column(k, r):
        rows = orb_n * block
        return out.at[pl.ds(pl.multiple_of(r * rows, rows), rows), columns(k)]

    def remote(src, dst, send, recv, device):
        return pltpu.make_async_remote_copy(
            src_ref=src, dst_ref=dst, send_sem=send, recv_sem=recv, device_id=device, device_id_type=MESH
        )

    def scatter(k, d):
        to = (z + d) % orb_n
        src = terms.at[k // split, pl.ds(pl.multiple_of(to * block, block), block), columns(k % split)]
        return remote(src, landed.at[k, d - 1], sum_s.at[k, d - 1], sum_r.at[k, d - 1], (row, to))

    def line(k, q, up, first=False):
        src = stage.at[k] if first else part(k, row, q)
        send = up_s.at[k, q] if up else down_s.at[k, q]
        return remote(src, part(k, row, q), send, line_r.at[k, q], (row, z + 1 if up else z - 1))

    def keep(k):
        return pltpu.make_async_copy(stage.at[k], part(k, row, z), local_s.at[k])

    def ring(k, hop, side):
        r = at(-(hop - 1)) if side == 0 else at(hop - 1)
        j = hop if side == 0 else chips - hop
        return remote(
            column(k, r), column(k, r), ring_s.at[k, side, hop - 1], ring_r.at[k, j],
            (onward if side == 0 else back, z),
        )

    def arrived(k, hop, side):
        r = at(-hop) if side == 0 else at(hop)
        j = hop if side == 0 else chips - hop
        remote(
            column(k, r), column(k, r), ring_s.at[k, side, hop - 1], ring_r.at[k, j],
            (onward if side == 0 else back, z),
        ).wait_recv()
        pair(k, j).start()

    def pair(k, j):
        r = at(-j)
        return remote(column(k, r), column(k, r), pair_s.at[k, j], pair_r.at[k, j], (other, z))

    def pair_in(k, j):
        r = at(-j) + 1 - 2 * core
        return remote(column(k, r), column(k, r), pair_s.at[k, j], pair_r.at[k, j], (other, z))

    hops = chips // 2

    def on_side(k, hop, side, act):
        if hop < hops:
            act()
        else:
            pl.when(k % 2 == side)(act)

    def total(k):
        rows = 32
        def one(i, carry):
            at_rows = pl.ds(pl.multiple_of(i * rows, rows), rows)
            value = own[k // split, at_rows, columns(k % split)]
            for d in range(orb_n - 1):
                value = value + landed[k, d, at_rows, :].astype(jnp.float32)
            stage[k, at_rows, :] = value.astype(jnp.bfloat16)
            return carry
        lax.fori_loop(0, block // rows, one, 0)

    for d in range(1, orb_n):
        scatter(0, d).start()

    def step(t, carry):
        before = t - 1

        @pl.when(t < chunks - 1)
        def _():
            for d in range(1, orb_n):
                scatter(t + 1, d).start()

        @pl.when(t < chunks)
        def _():
            for d in range(1, orb_n):
                scatter(t, d).wait_recv()
            total(t)
            keep(t).start()
            pl.when(z + 1 < orb_n)(lambda: line(t, z, True, True).start())
            pl.when(z >= 1)(lambda: line(t, z, False, True).start())

        @pl.when(t >= 1)
        def _():
            for hop in range(1, hops):
                for side in (0, 1):
                    arrived(before, hop, side)
                    on_side(before, hop + 1, side, lambda: ring(before, hop + 1, side).start())

        @pl.when(t < chunks)
        def _():
            for h in range(1, orb_n):
                @pl.when(z - h >= 0)
                def _():
                    line(t, z - h, True).wait_recv()
                    pl.when(z + 1 < orb_n)(lambda: line(t, z - h, True).start())

                @pl.when(z + h < orb_n)
                def _():
                    line(t, z + h, False).wait_recv()
                    pl.when(z >= 1)(lambda: line(t, z + h, False).start())
            keep(t).wait()
            for side in (0, 1):
                on_side(t, 1, side, lambda: ring(t, 1, side).start())
            pair(t, 0).start()

        @pl.when(t >= 1)
        def _():
            for side in (0, 1):
                on_side(before, hops, side, lambda: arrived(before, hops, side))

        return carry

    lax.fori_loop(0, chunks + 1, step, 0)

    def finish(k, carry):
        for d in range(1, orb_n):
            scatter(k, d).wait_send()
        for q in range(orb_n):
            pl.when(jnp.logical_and(z + 1 < orb_n, q <= z))(lambda: line(k, q, True).wait_send())
            pl.when(jnp.logical_and(z >= 1, q >= z))(lambda: line(k, q, False).wait_send())
        for hop in range(1, hops + 1):
            for side in (0, 1):
                on_side(k, hop, side, lambda: ring(k, hop, side).wait_send())
        for j in range(chips):
            pair(k, j).wait_send()
            pair_in(k, j).wait_recv()
        return carry

    lax.fori_loop(0, chunks, finish, 0)


def gather(terms, own, row_n, orb_n):
    vectors, rows, count = terms.shape
    block = rows // orb_n
    chips, chunks, width = row_n // CORES, vectors * SPLIT, count // SPLIT
    dma = pltpu.SemaphoreType.DMA
    return pl.pallas_call(
        functools.partial(gather_kernel, (row_n, orb_n, SPLIT)),
        out_shape=jax.ShapeDtypeStruct((row_n * rows, vectors * count), jnp.bfloat16),
        in_specs=[pl.BlockSpec(memory_space=pl.ANY), pl.BlockSpec(memory_space=pltpu.VMEM)],
        out_specs=pl.BlockSpec(memory_space=pl.ANY),
        scratch_shapes=[
            pltpu.VMEM((chunks, block, width), jnp.bfloat16),
            pltpu.VMEM((chunks, orb_n - 1, block, width), jnp.bfloat16),
            dma((chunks, orb_n - 1)),
            dma((chunks, orb_n - 1)),
            dma((chunks, orb_n)),
            dma((chunks, orb_n)),
            dma((chunks, orb_n)),
            dma((chunks, 2, chips // 2)),
            dma((chunks, chips)),
            dma((chunks, chips)),
            dma((chunks, chips)),
            dma((chunks,)),
        ],
        compiler_params=pltpu.CompilerParams(
            collective_id=0, has_side_effects=True, vmem_limit_bytes=50 * 1024 * 1024
        ),
    )(terms, own)


def on_device(chol_vectors, orbitals):
    row_n, orb_n = lax.axis_size("row"), lax.axis_size("orb")
    block = chol_vectors.shape[1] // orb_n

    def half_transform(vectors):
        return jnp.einsum("prm,mi->pri", vectors, orbitals, preferred_element_type=jnp.float32)

    terms = half_transform(chol_vectors).astype(jnp.bfloat16)
    z = lax.axis_index("orb")
    own = half_transform(lax.dynamic_slice_in_dim(chol_vectors, z * block, block, axis=1))
    whole = gather(terms, own, row_n, orb_n)
    place = (lax.axis_index("row") * orb_n + z) * block
    mine = lax.dynamic_slice_in_dim(whole, place, block, axis=0)
    return lax.dot_general(mine, whole, (((1,), (1,)), ((), ())), preferred_element_type=jnp.float32)


def solution(mesh):
    return jax.shard_map(
        on_device,
        mesh=mesh,
        in_specs=(P(None, "row", "orb"), P("orb", None)),
        out_specs=P(("row", "orb"), None),
        check_vma=False,
    )
```

```python
import functools

import jax
import jax.numpy as jnp
from jax import lax
from jax.experimental import pallas as pl
from jax.experimental.pallas import tpu as pltpu
from jax.sharding import PartitionSpec as P

MESH = pl.DeviceIdType.MESH
CORES = 2
SPLIT = 4


def snake(place, count):
    half = count // 2
    return place + (place // half) * (half + count - 1 - 2 * place)


def gather_kernel(
    sizes, vectors_ref, orbitals, out, held, terms, own, stage, landed, passing, load_s,
    sum_s, sum_r, pass_r, up_s, down_s, line_r, ring_s, ring_r, pair_s, pair_r, local_s,
):
    row_n, orb_n, split = sizes
    chips = row_n // CORES
    vectors, rows_n, depth = vectors_ref.shape
    count = orbitals.shape[1]
    block = rows_n // orb_n
    width = count // split
    chunks = vectors * split
    row, z = lax.axis_index("row"), lax.axis_index("orb")
    core = row % CORES
    place = snake(row // CORES, chips)

    def at(step):
        return snake((place + step + chips) % chips, chips) * CORES + core

    onward, back = at(1), at(-1)
    other = row + 1 - 2 * core

    barrier = pltpu.get_barrier_semaphore()
    peers = [(row, (z + d) % orb_n) for d in range(1, orb_n)]
    peers += [(onward, z), (back, z), (other, z)]
    for peer in peers:
        pl.semaphore_signal(barrier, inc=1, device_id=peer, device_id_type=MESH)
    pl.semaphore_wait(barrier, len(peers))

    def columns(k):
        return pl.ds(pl.multiple_of(k * width, width), width)

    def part(k, r, q):
        return out.at[pl.ds(pl.multiple_of((r * orb_n + q) * block, block), block), columns(k)]

    def column(k, r):
        rows = orb_n * block
        return out.at[pl.ds(pl.multiple_of(r * rows, rows), rows), columns(k)]

    def remote(src, dst, send, recv, device):
        return pltpu.make_async_remote_copy(
            src_ref=src, dst_ref=dst, send_sem=send, recv_sem=recv, device_id=device, device_id_type=MESH
        )

    def far(a, b):
        d = jnp.maximum(a - b, b - a)
        return jnp.logical_and(d >= 3, d % 2 == 1)

    def relays(o):
        d = jnp.maximum(z - o, o - z)
        outer = jnp.logical_or(
            jnp.logical_and(z > o, z + 1 < orb_n), jnp.logical_and(z < o, z >= 1)
        )
        return jnp.logical_and(jnp.logical_and(d >= 2, d % 2 == 0), outer)

    def to_owner(k, o):
        return remote(terms.at[k, o], landed.at[k, z], sum_s.at[k, o], sum_r.at[k, z], (row, o))

    def to_relay(k, o):
        nearer = jnp.where(z > o, z - 1, z + 1)
        return remote(terms.at[k, o], passing.at[k, o], sum_s.at[k, o], pass_r.at[k, o], (row, nearer))

    def from_source(k, q):
        return remote(terms.at[k, q], landed.at[k, q], sum_s.at[k, q], sum_r.at[k, q], (row, q))

    def from_outer(k, o):
        return remote(terms.at[k, o], passing.at[k, o], sum_s.at[k, o], pass_r.at[k, o], (row, o))

    def relay(k):
        for o in range(orb_n):
            @pl.when(relays(o))
            def _():
                from_outer(k, o).wait_recv()
                rows = 32

                def one(i, carry):
                    at_rows = pl.ds(pl.multiple_of(i * rows, rows), rows)
                    value = own[k % 2, o, at_rows, :] + passing[k, o, at_rows, :].astype(jnp.float32)
                    terms[k, o, at_rows, :] = value.astype(jnp.bfloat16)
                    return carry

                lax.fori_loop(0, block // rows, one, 0)
                to_owner(k, o).start()

    def line(k, q, up, first=False):
        src = stage.at[k] if first else part(k, row, q)
        send = up_s.at[k, q] if up else down_s.at[k, q]
        return remote(src, part(k, row, q), send, line_r.at[k, q], (row, z + 1 if up else z - 1))

    def keep(k):
        return pltpu.make_async_copy(stage.at[k], part(k, row, z), local_s.at[k])

    def ring(k, hop, side):
        r = at(-(hop - 1)) if side == 0 else at(hop - 1)
        j = hop if side == 0 else chips - hop
        return remote(
            column(k, r), column(k, r), ring_s.at[k, side, hop - 1], ring_r.at[k, j],
            (onward if side == 0 else back, z),
        )

    def arrived(k, hop, side):
        r = at(-hop) if side == 0 else at(hop)
        j = hop if side == 0 else chips - hop
        remote(
            column(k, r), column(k, r), ring_s.at[k, side, hop - 1], ring_r.at[k, j],
            (onward if side == 0 else back, z),
        ).wait_recv()
        pair(k, j).start()

    def pair(k, j):
        r = at(-j)
        return remote(column(k, r), column(k, r), pair_s.at[k, j], pair_r.at[k, j], (other, z))

    def pair_in(k, j):
        r = at(-j) + 1 - 2 * core
        return remote(column(k, r), column(k, r), pair_s.at[k, j], pair_r.at[k, j], (other, z))

    hops = chips // 2

    def on_side(k, hop, side, act):
        if hop < hops:
            act()
        else:
            pl.when(k % 2 == side)(act)

    def takes(q):
        return jnp.logical_and(z != q, jnp.logical_not(far(q, z)))

    def total(k):
        rows = 32

        def add(q):
            def one(i, carry):
                at_rows = pl.ds(pl.multiple_of(i * rows, rows), rows)
                own[k % 2, z, at_rows, :] += landed[k, q, at_rows, :].astype(jnp.float32)
                return carry

            lax.fori_loop(0, block // rows, one, 0)

        for q in range(orb_n):
            @pl.when(takes(q))
            def _():
                from_source(k, q).wait_recv()
                add(q)

        def one(i, carry):
            at_rows = pl.ds(pl.multiple_of(i * rows, rows), rows)
            stage[k, at_rows, :] = own[k % 2, z, at_rows, :].astype(jnp.bfloat16)
            return carry

        lax.fori_loop(0, block // rows, one, 0)

    def load(p):
        return pltpu.make_async_copy(vectors_ref.at[p], held.at[p % 2], load_s.at[p % 2])

    def begin(k):
        p = k // split

        @pl.when(k % split == 0)
        def _():
            load(p).wait()
            pl.when(p + 1 < vectors)(lambda: load(p + 1).start())

        def one(q, carry):
            value = jnp.dot(
                held[p % 2, pl.ds(pl.multiple_of(q * block, block), block), :],
                orbitals[:, columns(k % split)],
                preferred_element_type=jnp.float32,
            )
            terms[k, q] = value.astype(jnp.bfloat16)
            own[k % 2, q] = value

            return carry

        lax.fori_loop(0, orb_n, one, 0)
        for o in range(orb_n):
            pl.when(far(o, z))(lambda: to_relay(k, o).start())
        for o in range(orb_n):
            near = jnp.logical_and(takes(o), jnp.logical_not(relays(o)))
            pl.when(near)(lambda: to_owner(k, o).start())

    load(0).start()
    begin(0)
    relay(0)

    def step(t, carry):
        @pl.when(t < chunks)
        def _():
            total(t)
            keep(t).start()
            pl.when(z + 1 < orb_n)(lambda: line(t, z, True, True).start())
            pl.when(z >= 1)(lambda: line(t, z, False, True).start())

        pl.when(t < chunks - 1)(lambda: begin(t + 1))

        @pl.when(t < chunks)
        def _():
            for h in range(1, orb_n):
                @pl.when(z - h >= 0)
                def _():
                    line(t, z - h, True).wait_recv()
                    pl.when(z + 1 < orb_n)(lambda: line(t, z - h, True).start())

                @pl.when(z + h < orb_n)
                def _():
                    line(t, z + h, False).wait_recv()
                    pl.when(z >= 1)(lambda: line(t, z + h, False).start())
            keep(t).wait()
            for side in (0, 1):
                on_side(t, 1, side, lambda: ring(t, 1, side).start())
            pair(t, 0).start()

        pl.when(t < chunks - 1)(lambda: relay(t + 1))

        @pl.when(jnp.logical_and(t >= 1, t <= chunks))
        def _():
            for hop in range(1, hops):
                for side in (0, 1):
                    arrived(t - 1, hop, side)
                    on_side(t - 1, hop + 1, side, lambda: ring(t - 1, hop + 1, side).start())

        @pl.when(t >= 2)
        def _():
            for side in (0, 1):
                on_side(t - 2, hops, side, lambda: arrived(t - 2, hops, side))

        return carry

    lax.fori_loop(0, chunks + 2, step, 0)

    def finish(k, carry):
        for o in range(orb_n):
            pl.when(far(o, z))(lambda: to_relay(k, o).wait_send())
            pl.when(takes(o))(lambda: to_owner(k, o).wait_send())
        for q in range(orb_n):
            pl.when(jnp.logical_and(z + 1 < orb_n, q <= z))(lambda: line(k, q, True).wait_send())
            pl.when(jnp.logical_and(z >= 1, q >= z))(lambda: line(k, q, False).wait_send())
        for hop in range(1, hops + 1):
            for side in (0, 1):
                on_side(k, hop, side, lambda: ring(k, hop, side).wait_send())
        for j in range(chips):
            pair(k, j).wait_send()
            pair_in(k, j).wait_recv()
        return carry

    lax.fori_loop(0, chunks, finish, 0)


def gather(chol_vectors, orbitals, row_n, orb_n):
    vectors, rows, depth = chol_vectors.shape
    count = orbitals.shape[1]
    block = rows // orb_n
    chips, chunks, width = row_n // CORES, vectors * SPLIT, count // SPLIT
    dma = pltpu.SemaphoreType.DMA
    return pl.pallas_call(
        functools.partial(gather_kernel, (row_n, orb_n, SPLIT)),
        out_shape=jax.ShapeDtypeStruct((row_n * rows, vectors * count), jnp.bfloat16),
        in_specs=[pl.BlockSpec(memory_space=pl.ANY), pl.BlockSpec(memory_space=pltpu.VMEM)],
        out_specs=pl.BlockSpec(memory_space=pl.ANY),
        scratch_shapes=[
            pltpu.VMEM((2, rows, depth), jnp.bfloat16),
            pltpu.VMEM((chunks, orb_n, block, width), jnp.bfloat16),
            pltpu.VMEM((2, orb_n, block, width), jnp.float32),
            pltpu.VMEM((chunks, block, width), jnp.bfloat16),
            pltpu.VMEM((chunks, orb_n, block, width), jnp.bfloat16),
            pltpu.VMEM((chunks, orb_n, block, width), jnp.bfloat16),
            dma((2,)),
            dma((chunks, orb_n)),
            dma((chunks, orb_n)),
            dma((chunks, orb_n)),
            dma((chunks, orb_n)),
            dma((chunks, orb_n)),
            dma((chunks, orb_n)),
            dma((chunks, 2, chips // 2)),
            dma((chunks, chips)),
            dma((chunks, chips)),
            dma((chunks, chips)),
            dma((chunks,)),
        ],
        compiler_params=pltpu.CompilerParams(
            collective_id=0, has_side_effects=True, vmem_limit_bytes=56 * 1024 * 1024
        ),
    )(chol_vectors, orbitals)


def on_device(chol_vectors, orbitals):
    row_n, orb_n = lax.axis_size("row"), lax.axis_size("orb")
    block = chol_vectors.shape[1] // orb_n

    z = lax.axis_index("orb")
    whole = gather(chol_vectors, orbitals, row_n, orb_n)
    place = (lax.axis_index("row") * orb_n + z) * block
    mine = lax.dynamic_slice_in_dim(whole, place, block, axis=0)
    return lax.dot_general(mine, whole, (((1,), (1,)), ((), ())), preferred_element_type=jnp.float32)


def solution(mesh):
    return jax.shard_map(
        on_device,
        mesh=mesh,
        in_specs=(P(None, "row", "orb"), P("orb", None)),
        out_specs=P(("row", "orb"), None),
        check_vma=False,
    )
```
